32 devices in a mesh: groups: 2 (over y), blk: 16 (over z, x, core).
Axes of the slice: x: 2, y: 2, z: 4, core: 2. Of those that a mesh axis runs over, the one named last changes fastest.
Arguments:
- queries: bfloat16 [16384, 2048], P(('groups', 'blk')), parts along dimension 0, may hold values from -6 to 6
- gallery: bfloat16 [49152, 2048], P(('groups', 'blk')), parts along dimension 0, may hold values from -6 to 6
- neighbors: int32 [16384, 4, 8], P(('groups', 'blk')), parts along dimension 0, may hold values from 0 to 1535
- counts: int32 [32], P(('groups', 'blk')), parts along dimension 0, may hold values from 768 to 1536, as said below
Outputs:
- expanded: bfloat16 [16384, 2048], P(('groups', 'blk')), parts along dimension 0
The draws below stay inside these ranges and needn't reach their ends.
There are 2 independent parts, one for each index of `groups`. The reference program is written for one: setup_inputs(seed, part) draws one part's arguments, and reference() takes and returns one part's arrays. A program takes and returns all parts, laid end to end along the dimension named above; each array names one. Nothing has to cross between parts.
Inputs may be any that keep to these rules, and one draw needn't show every extreme that they name: `counts`: the largest count equals 1536 in every draw.
All inputs are finite; a program needn't handle non-finite values.
Results may differ from the reference program's by a relative error of at most 0.0085.
Values may be sent and summed in bfloat16 or wider, within the bound.
No kernel may reach another device: no remote copies, remote signals or barrier semaphores. Data moves between devices by JAX's collectives and lax.ppermute only.
A program may use at most 192 MiB of HBM per device.

```python
import jax
import jax.numpy as jnp
from jax import lax

D = 2048
Q_DEV = 512
GAL_DEV = 1536
STEPS = 4
TOPK = 8
N_BLK_ALL = 16
QUERIES = 8192
GALLERY = 24576


def draw_counts(key, part):
    key = jax.random.fold_in(key, 11)
    first, second = jax.random.split(key)
    base = jax.random.randint(first, (N_BLK_ALL,), GAL_DEV // 2, GAL_DEV + 1)
    place = jax.random.randint(second, (), 0, N_BLK_ALL)
    spots = jnp.arange(N_BLK_ALL)
    return jnp.where(spots == place, GAL_DEV, base).astype(jnp.int32)


def with_ends(entries, key, low, top_value):
    longest = entries.shape.index(max(entries.shape))
    spots = []
    for shift in (0, 1):
        where = [jax.random.randint(jax.random.fold_in(key, axis), (), 0, length) for axis, length in enumerate(entries.shape)]
        where[longest] = (where[longest] + shift) % entries.shape[longest]
        spots.append(tuple(where))
    return entries.at[spots[0]].set(low).at[spots[1]].set(top_value)


def block_levels(own_key, shape, pieces, least, largest):
    gain = 1.0
    for position, parts in pieces:
        steps = jax.random.uniform(jax.random.fold_in(jax.random.fold_in(own_key, 6), position), (parts,), jnp.float32, least / len(pieces), largest / len(pieces))
        gain = gain * jnp.repeat(jnp.exp(steps), shape[position] // parts).reshape((-1,) + (1,) * (len(shape) - 1 - position))
    return gain


def gaussian(stream_key, extent, deviation, limit, cuts=(), kind=jnp.bfloat16):
    drawn = jax.random.normal(stream_key, extent, jnp.float32) * deviation
    if len(cuts) > 0:
        drawn = block_levels(stream_key, extent, cuts, -0.22, 0.18) * drawn
    return jnp.clip(drawn, min=-limit, max=limit).astype(kind)


def setup_inputs(seed: int = 0, part: int = 0) -> dict:
    streams_of = jax.random.split(jax.random.key(seed), 5)
    own_keys = jax.random.split(jax.random.fold_in(streams_of[4], part), 5)
    return {
        "queries": gaussian(own_keys[0], (QUERIES, D), 1.0, 6.0, ((0, 16),)),
        "gallery": gaussian(own_keys[1], (GALLERY, D), 1.0, 6.0, ((0, 16),)),
        "neighbors": with_ends(jax.random.randint(own_keys[2], (QUERIES, STEPS, TOPK), 0, GAL_DEV), jax.random.fold_in(own_keys[2], 1), 0, GAL_DEV - 1).astype(jnp.int32),
        "counts": draw_counts(jax.random.fold_in(jax.random.fold_in(streams_of[4], part), 71), part),
    }


def reference(queries, gallery, neighbors, counts):
    scale = 1.0 / (D ** 0.5)
    earlier = (lax.broadcasted_iota(jnp.int32, (TOPK, TOPK), 1) < lax.broadcasted_iota(jnp.int32, (TOPK, TOPK), 0))

    def one_block(anchor):
        query_rows = lax.dynamic_slice_in_dim(queries, anchor * Q_DEV, Q_DEV, 0)
        index_rows = lax.dynamic_slice_in_dim(neighbors, anchor * Q_DEV, Q_DEV, 0)
        query_f = query_rows.astype(jnp.float32)
        total = jnp.zeros((Q_DEV, D), jnp.float32)
        mass = jnp.zeros((Q_DEV,), jnp.float32)
        for step in range(STEPS):
            target = ((anchor + step) % N_BLK_ALL).astype(jnp.int32)
            block = lax.dynamic_slice_in_dim(gallery, target * GAL_DEV, GAL_DEV, 0)
            live = counts[target]
            picks = index_rows[:, step, :]
            rows = block[picks].astype(jnp.float32)
            score = jnp.einsum("qd,qkd->qk", query_f, rows) * scale
            relu_s = jnp.maximum(score, 0.0)
            weight = relu_s * relu_s * relu_s * (picks < live).astype(jnp.float32)
            same = picks[:, :, None] == picks[:, None, :]
            summed = jnp.sum(jnp.where(same, weight[:, None, :], 0.0), axis=2)
            repeat = jnp.any(same & earlier[None, :, :], axis=2)
            first = jnp.where(repeat, 0.0, 1.0)
            weight_b = summed.astype(jnp.bfloat16).astype(jnp.float32) * first
            total = total + jnp.einsum("qk,qkd->qd", weight_b, rows)
            mass = mass + jnp.sum(weight, axis=1)
        return ((query_f + total) / (1.0 + mass)[:, None]).astype(jnp.bfloat16)

    result = lax.map(one_block, jnp.arange(N_BLK_ALL, dtype=jnp.int32))
    return result.reshape(QUERIES, D)
```

```python
import functools

import jax
import jax.numpy as jnp
from jax import lax
from jax.experimental import pallas as pl
from jax.experimental.pallas import tpu as pltpu
from jax.sharding import PartitionSpec as P

CHUNKS = 2
TILE = 256
NO_PICK = 4095


def meet_kernel(n_gal, topk, scale3, live_ref, q_ref, enc_ref, *refs):
    gal_refs = refs[:n_gal]
    out_ref, mass_ref, w_ref = refs[n_gal:]
    rows = q_ref.shape[0]
    gal_rows, width = gal_refs[0].shape
    q = q_ref[...]
    mass = jnp.zeros((rows, 128), jnp.float32)
    for g in range(n_gal):
        live = live_ref[g]
        enc = enc_ref[:, g * topk : (g + 1) * topk]
        pick = enc & NO_PICK
        pick = jnp.where(pick < live, pick, -1)
        gain = (enc >> 12).astype(jnp.float32) * scale3
        for t in range(gal_rows // TILE):
            tile = gal_refs[g][t * TILE : (t + 1) * TILE, :]
            s = lax.dot_general(q, tile, (((1,), (1,)), ((), ())), preferred_element_type=jnp.float32)
            col = lax.broadcasted_iota(jnp.int32, (rows, TILE), 1) + t * TILE
            c = jnp.zeros((rows, TILE), jnp.float32)
            for k in range(topk):
                c = jnp.where(col == pick[:, k : k + 1], gain[:, k : k + 1], c)
            r = jnp.maximum(s, 0.0)
            w = r * r * (r * c)
            for j in range(TILE // 128):
                mass = mass + w[:, j * 128 : (j + 1) * 128]
            w_ref[g, :, t * TILE : (t + 1) * TILE] = w.astype(jnp.bfloat16)
    mass_ref[...] = jnp.sum(mass, axis=1, keepdims=True)
    for n in range(width // TILE):
        cut = slice(n * TILE, (n + 1) * TILE)
        total = jnp.dot(w_ref[0], gal_refs[0][:, cut], preferred_element_type=jnp.float32)
        for g in range(1, n_gal):
            total = total + jnp.dot(w_ref[g], gal_refs[g][:, cut], preferred_element_type=jnp.float32)
        out_ref[:, cut] = total.astype(out_ref.dtype)


def meet(q, enc, lives, gals, topk, row_block=256):
    rows, width = q.shape
    gal_rows = gals[0].shape[0]
    n_gal = len(gals)
    row_block = min(row_block, rows)
    vmem = pltpu.VMEM
    return pl.pallas_call(
        functools.partial(meet_kernel, n_gal, topk, float(width) ** -1.5),
        grid=(rows // row_block,),
        out_shape=(
            jax.ShapeDtypeStruct((rows, width), jnp.bfloat16),
            jax.ShapeDtypeStruct((rows, 1), jnp.float32),
        ),
        in_specs=[
            pl.BlockSpec(memory_space=pltpu.SMEM),
            pl.BlockSpec((row_block, width), lambda i: (i, 0)),
            pl.BlockSpec((row_block, n_gal * topk), lambda i: (i, 0)),
        ]
        + [pl.BlockSpec((gal_rows, width), lambda i: (0, 0))] * n_gal,
        out_specs=(
            pl.BlockSpec((row_block, width), lambda i: (i, 0)),
            pl.BlockSpec((row_block, 1), lambda i: (i, 0)),
        ),
        scratch_shapes=[vmem((n_gal, row_block, gal_rows), jnp.bfloat16)],
        compiler_params=pltpu.CompilerParams(vmem_limit_bytes=56 * 1024 * 1024),
        cost_estimate=pl.CostEstimate(
            flops=4 * rows * gal_rows * width * n_gal,
            bytes_accessed=2 * n_gal * gal_rows * width + 4 * rows * width,
            transcendentals=0,
        ),
    )(lives, q, enc, *gals)


def on_device(queries, gallery, neighbors, counts):
    n = lax.axis_size("blk")
    core = lax.axis_index("blk") % 2
    rows, width = queries.shape
    topk = neighbors.shape[2]

    def shift(k):
        return [(i, (i + k) % n) for i in range(n)]

    def odd_shift(k):
        return [(i, (i + k) % n if i % 2 else i) for i in range(n)]

    swap = [(i, i ^ 1) for i in range(n)]

    same = neighbors[:, :, :, None] == neighbors[:, :, None, :]
    many = jnp.sum(same.astype(jnp.int32), axis=3)
    order = jnp.arange(topk)
    repeat = jnp.any(same & (order[None, :] < order[:, None]), axis=3)
    enc = jnp.where(repeat, NO_PICK, neighbors + (many << 12))
    enc_own = enc[:, 0]
    enc_near = jnp.concatenate([enc[:, 2], jnp.where(core == 0, enc[:, 3], enc[:, 1])], axis=1)
    enc_far = jnp.where(core == 0, enc[:, 1], enc[:, 3])

    size = rows // CHUNKS
    near = [lax.ppermute(queries[c * size : (c + 1) * size], "blk", shift(2)) for c in range(CHUNKS)]
    enc_near = lax.ppermute(enc_near.T, "blk", shift(2)).T
    enc_far = lax.ppermute(enc_far.T, "blk", odd_shift(4)).T
    far = lax.ppermute(queries, "blk", odd_shift(4))
    other = lax.ppermute(gallery, "blk", swap)
    live = jnp.concatenate([counts, lax.ppermute(counts, "blk", swap)])

    total_own, mass_own = meet(queries, enc_own, live[:1], (gallery,), topk)
    total_far, mass_far = meet(far, enc_far, live[1:], (other,), topk)
    total_far = lax.ppermute(total_far, "blk", odd_shift(-4))
    mass_far = lax.ppermute(mass_far[:, 0], "blk", odd_shift(-4))
    outs = []
    for c in range(CHUNKS):
        cut = slice(c * size, (c + 1) * size)
        total, mass = meet(near[c], enc_near[cut], live, (gallery, other), topk)
        total = lax.ppermute(total, "blk", shift(-2))
        mass = lax.ppermute(mass[:, 0], "blk", shift(-2))
        mass = mass + mass_own[cut, 0] + mass_far[cut]
        sums = queries[cut].astype(jnp.float32) + total_own[cut] + total_far[cut] + total
        outs.append((sums / (1.0 + mass)[:, None]).astype(jnp.bfloat16))
    return jnp.concatenate(outs, axis=0)


def solution(mesh):
    return jax.shard_map(
        on_device,
        mesh=mesh,
        in_specs=(
            P(("groups", "blk"), None),
            P(("groups", "blk"), None),
            P(("groups", "blk"), None, None),
            P(("groups", "blk")),
        ),
        out_specs=P(("groups", "blk"), None),
        check_vma=False,
    )
```

```python
import functools

import jax
import jax.numpy as jnp
from jax import lax
from jax.experimental import pallas as pl
from jax.experimental.pallas import tpu as pltpu
from jax.sharding import PartitionSpec as P

CHUNKS = 2
ORDER = (("near", 0), ("far", 0), ("far", 1), ("near", 1))
TILE = 256
TAIL = 16
BASE = 256
VMEM_BYTES = 65000 * 1024


def cost(flops):
    return pl.CostEstimate(flops=flops, bytes_accessed=flops // 64, transcendentals=0)


def pack_kernel(q_ref, picks_ref, out_ref):
    steps, topk, rows = picks_ref.shape
    out_ref[:rows, :] = q_ref[...]
    out_ref[rows:, :] = jnp.zeros((TAIL, out_ref.shape[1]), out_ref.dtype)
    for s in range(steps):
        picks = picks_ref[s]
        halves = [(picks >> 8).astype(jnp.float32), (picks & (BASE - 1)).astype(jnp.float32)]
        out_ref[rows:, s * rows : (s + 1) * rows] = jnp.concatenate(halves, axis=0).astype(out_ref.dtype)


def pack(queries, picks, first, rows):
    width = queries.shape[1]
    at = first // rows
    return pl.pallas_call(
        pack_kernel,
        grid=(1,),
        out_shape=jax.ShapeDtypeStruct((rows + TAIL, width), queries.dtype),
        in_specs=[
            pl.BlockSpec((rows, width), lambda i: (at, 0)),
            pl.BlockSpec((*picks.shape[:2], rows), lambda i: (0, 0, at)),
        ],
        out_specs=pl.BlockSpec((rows + TAIL, width), lambda i: (0, 0)),
        compiler_params=pltpu.CompilerParams(vmem_limit_bytes=VMEM_BYTES),
        cost_estimate=cost(rows * width),
    )(queries, picks)


def unpack(tail, topk):
    parts = tail.astype(jnp.float32)
    return (parts[:topk] * BASE + parts[topk:]).astype(jnp.int32)


def pick_table(picks, live, scale3):
    topk = picks.shape[0]
    place = lax.broadcasted_iota(jnp.int32, picks.shape, 0)
    many = jnp.ones(picks.shape, jnp.float32)
    keep = picks < live
    for turn in range(1, topk):
        same = picks == pltpu.roll(picks, turn, 0)
        many = many + jnp.where(same, 1.0, 0.0)
        keep = keep & jnp.logical_not(same & (place >= turn))
    return jnp.where(keep, picks, -1).T, (many * scale3).T


def meet_kernel(n_src, gal_ids, scale3, topk, core_ref, live_ref, token_ref, *refs):
    n_gal = len(gal_ids)
    even = core_ref[0] == 0
    sources = [refs[i * (1 + 2 * n_gal) : (i + 1) * (1 + 2 * n_gal)] for i in range(n_src)]
    refs = refs[n_src * (1 + 2 * n_gal) :]
    gal_refs, refs = refs[:n_gal], refs[n_gal:]
    out_ref, w_ref = refs[:2]
    q_ref = sources[0][0]
    rows = q_ref.shape[0]
    if n_src == 2:
        far_ref, q_ref = sources[1][0], refs[2]

        @pl.when(even)
        def _():
            q_ref[...] = sources[0][0][...]

        @pl.when(jnp.logical_not(even))
        def _():
            q_ref[...] = far_ref[...]

    gal_rows, width = gal_refs[0].shape
    mass = jnp.zeros((rows, 128), jnp.float32)
    for g in range(n_gal):
        first, last = sources[0][1 + 2 * g], sources[-1][2 + 2 * g]
        if len(first.shape) == 3:
            picks = first[0]
        else:
            picks = jnp.where(even, unpack(first[...], topk), unpack(last[...], topk))
        pick, gain = pick_table(picks, live_ref[gal_ids[g]], scale3)
        for t in range(gal_rows // TILE):
            tile = gal_refs[g][t * TILE : (t + 1) * TILE, :]
            s = lax.dot_general(q_ref[...], tile, (((1,), (1,)), ((), ())), preferred_element_type=jnp.float32)
            col = lax.broadcasted_iota(jnp.int32, (rows, TILE), 1) + t * TILE
            c = jnp.zeros((rows, TILE), jnp.float32)
            for k in range(topk):
                c = jnp.where(col == pick[:, k : k + 1], gain[:, k : k + 1], c)
            r = jnp.maximum(s, 0.0)
            w = r * r * (r * c)
            for j in range(TILE // 128):
                mass = mass + w[:, j * 128 : (j + 1) * 128]
            w_ref[g, :, t * TILE : (t + 1) * TILE] = w.astype(jnp.bfloat16)
    for n in range(width // TILE):
        cut = slice(n * TILE, (n + 1) * TILE)
        total = jnp.dot(w_ref[0], gal_refs[0][:, cut], preferred_element_type=jnp.float32)
        for g in range(1, n_gal):
            total = total + jnp.dot(w_ref[g], gal_refs[g][:, cut], preferred_element_type=jnp.float32)
        out_ref[:rows, cut] = total.astype(out_ref.dtype)
    mass = jnp.sum(mass.T, axis=0, keepdims=True)
    high = mass.astype(jnp.bfloat16).astype(jnp.float32)
    mid = (mass - high).astype(jnp.bfloat16).astype(jnp.float32)
    part = lax.broadcasted_iota(jnp.int32, (TAIL, rows), 0)
    tail = jnp.where(part == 0, high, jnp.where(part == 1, mid, jnp.where(part == 2, mass - high - mid, 0.0)))
    out_ref[rows:, :] = jnp.zeros((TAIL, width), out_ref.dtype)
    out_ref[rows:, :rows] = tail.astype(out_ref.dtype)


def meet(core, lives, token, sources, gals, steps, rows, at, topk):
    gal_rows, width = gals[0].shape
    n_gal = len(gals)
    operands, specs = [], []
    for source in sources:
        raw = isinstance(source, tuple)
        queries = source[0] if raw else source
        operands.append(queries)
        specs.append(pl.BlockSpec((rows, width), functools.partial(lambda o, i: (o, 0), at if raw else 0)))
        for _, *both in steps:
            for step in both:
                if raw:
                    operands.append(source[1])
                    specs.append(pl.BlockSpec((1, topk, rows), functools.partial(lambda s, i: (s, 0, at), step)))
                else:
                    operands.append(queries)
                    specs.append(
                        pl.BlockSpec((TAIL, rows), functools.partial(lambda s, i: (rows // TAIL, s), step))
                    )
    scratch = [pltpu.VMEM((n_gal, rows, gal_rows), jnp.bfloat16)]
    if len(sources) == 2:
        scratch.append(pltpu.VMEM((rows, width), jnp.bfloat16))
    return pl.pallas_call(
        functools.partial(meet_kernel, len(sources), tuple(s[0] for s in steps), float(width) ** -1.5, topk),
        grid=(1,),
        out_shape=jax.ShapeDtypeStruct((rows + TAIL, width), jnp.bfloat16),
        in_specs=[
            pl.BlockSpec(memory_space=pltpu.SMEM),
            pl.BlockSpec(memory_space=pltpu.SMEM),
            pl.BlockSpec(memory_space=pl.ANY),
        ]
        + specs
        + [pl.BlockSpec((gal_rows, width), lambda i: (0, 0))] * n_gal,
        out_specs=pl.BlockSpec((rows + TAIL, width), lambda i: (0, 0)),
        scratch_shapes=scratch,
        compiler_params=pltpu.CompilerParams(vmem_limit_bytes=VMEM_BYTES),
        cost_estimate=cost(rows * width),
    )(core, lives, token, *operands, *gals)


def finish_kernel(core_ref, q_ref, own_ref, own_tail, near_ref, near_tail, far_ref, far_tail, back_ref, back_tail, *refs):
    out_ref = refs[-1]
    rows = q_ref.shape[0]
    even = core_ref[0] == 0

    def write(far_ref, far_tail):
        tails = own_tail[...].astype(jnp.float32) + near_tail[...].astype(jnp.float32) + far_tail[...].astype(jnp.float32)
        mass = 1.0 + jnp.sum(tails.T, axis=1, keepdims=True)
        total = own_ref[...].astype(jnp.float32) + near_ref[...].astype(jnp.float32) + far_ref[...].astype(jnp.float32)
        out_ref[...] = ((q_ref[...].astype(jnp.float32) + total) / mass).astype(out_ref.dtype)

    @pl.when(even)
    def _():
        write(far_ref, far_tail)

    @pl.when(jnp.logical_not(even))
    def _():
        write(back_ref, back_tail)


def finish(core, at, rows, queries, own, near, far, back, done, block=128):
    width = queries.shape[1]
    per = rows // block
    first = at * per
    operands, specs = [queries], [pl.BlockSpec((block, width), lambda i: (first + i, 0))]
    for array, begin in ((own, first), (near, 0), (far, 0), (back, 0)):
        tail_row = (array.shape[0] - TAIL) // TAIL
        operands += [array, array]
        specs.append(pl.BlockSpec((block, width), functools.partial(lambda o, i: (o + i, 0), begin)))
        specs.append(pl.BlockSpec((TAIL, block), functools.partial(lambda t, o, i: (t, o + i), tail_row, begin)))
    extra = {}
    if done is not None:
        operands.append(done)
        specs.append(pl.BlockSpec(memory_space=pl.ANY))
        extra = {"input_output_aliases": {len(operands): 0}}
    return pl.pallas_call(
        finish_kernel,
        grid=(per,),
        out_shape=jax.ShapeDtypeStruct(queries.shape, queries.dtype),
        in_specs=[pl.BlockSpec(memory_space=pltpu.SMEM)] + specs,
        out_specs=pl.BlockSpec((block, width), lambda i: (first + i, 0)),
        compiler_params=pltpu.CompilerParams(vmem_limit_bytes=VMEM_BYTES),
        cost_estimate=cost(rows * width),
        **extra,
    )(core, *operands)


def on_device(queries, gallery, neighbors, counts):
    n = lax.axis_size("blk")
    core = jnp.reshape(lax.axis_index("blk") % 2, (1,)).astype(jnp.int32)
    rows, width = queries.shape
    topk = neighbors.shape[2]
    picks = jnp.transpose(neighbors, (1, 2, 0))

    def shift(k):
        return [(i, (i + k) % n) for i in range(n)]

    def odd_shift(k):
        return [(i, (i + k) % n) for i in range(1, n, 2)]

    swap = [(i, i ^ 1) for i in range(n)]

    size = rows // CHUNKS
    packed = [pack(queries, picks, c * size, size) for c in range(CHUNKS)]
    near = [lax.ppermute(chunk, "blk", shift(2)) for chunk in packed]
    other = lax.ppermute(gallery, "blk", swap)
    live = jnp.concatenate([counts, lax.ppermute(counts, "blk", swap)])
    far = [lax.ppermute(chunk, "blk", odd_shift(4)) for chunk in packed]

    own = meet(core, counts, packed[-1], [(queries, picks)], (gallery,), ((0, 0, 0),), rows, 0, topk)
    token = own
    near_back, far_here, far_back = {}, {}, {}
    for kind, c in ORDER:
        if kind == "near":
            token = meet(core, live, token, [near[c]], (gallery, other), ((0, 2, 2), (1, 3, 1)), size, 0, topk)
            near_back[c] = lax.ppermute(token, "blk", shift(-2))
        else:
            token = meet(core, live, token, [packed[c], far[c]], (other,), ((1, 1, 3),), size, 0, topk)
            far_here[c] = token
            far_back[c] = lax.ppermute(token, "blk", odd_shift(-4))
    done = None
    for c in range(CHUNKS):
        done = finish(core, c, size, queries, own, near_back[c], far_here[c], far_back[c], done)
    return done


def solution(mesh):
    return jax.shard_map(
        on_device,
        mesh=mesh,
        in_specs=(
            P(("groups", "blk"), None),
            P(("groups", "blk"), None),
            P(("groups", "blk"), None, None),
            P(("groups", "blk")),
        ),
        out_specs=P(("groups", "blk"), None),
        check_vma=False,
    )
```

```python
import functools

import jax
import jax.numpy as jnp
from jax import lax
from jax.experimental import pallas as pl
from jax.experimental.pallas import tpu as pltpu
from jax.sharding import PartitionSpec as P

CHUNKS = 2
TILE = 256
TAIL = 16
BASE = 256
VMEM_BYTES = 65000 * 1024


def cost(flops):
    return pl.CostEstimate(flops=flops, bytes_accessed=flops // 64, transcendentals=0)


def pack_kernel(q_ref, picks_ref, token_ref, out_ref):
    steps, topk, rows = picks_ref.shape
    out_ref[:rows, :] = q_ref[...]
    out_ref[rows:, :] = jnp.zeros((TAIL, out_ref.shape[1]), out_ref.dtype)
    for s in range(steps):
        picks = picks_ref[s]
        halves = [(picks >> 8).astype(jnp.float32), (picks & (BASE - 1)).astype(jnp.float32)]
        out_ref[rows:, s * rows : (s + 1) * rows] = jnp.concatenate(halves, axis=0).astype(out_ref.dtype)


def pack(queries, picks, token, first, rows):
    width = queries.shape[1]
    at = first // rows
    return pl.pallas_call(
        pack_kernel,
        grid=(1,),
        out_shape=jax.ShapeDtypeStruct((rows + TAIL, width), queries.dtype),
        in_specs=[
            pl.BlockSpec((rows, width), lambda i: (at, 0)),
            pl.BlockSpec((*picks.shape[:2], rows), lambda i: (0, 0, at)),
            pl.BlockSpec(memory_space=pl.ANY),
        ],
        out_specs=pl.BlockSpec((rows + TAIL, width), lambda i: (0, 0)),
        compiler_params=pltpu.CompilerParams(vmem_limit_bytes=VMEM_BYTES),
        cost_estimate=cost(rows * width),
    )(queries, picks, token)


def unpack(tail, topk):
    parts = tail.astype(jnp.float32)
    return (parts[:topk] * BASE + parts[topk:]).astype(jnp.int32)


def pick_table(picks, live, scale3):
    topk = picks.shape[0]
    place = lax.broadcasted_iota(jnp.int32, picks.shape, 0)
    many = jnp.ones(picks.shape, jnp.float32)
    keep = picks < live
    for turn in range(1, topk):
        same = picks == pltpu.roll(picks, turn, 0)
        many = many + jnp.where(same, 1.0, 0.0)
        keep = keep & jnp.logical_not(same & (place >= turn))
    return jnp.where(keep, picks, -1).T, (many * scale3).T


def meet_kernel(active, n_token, *rest):
    rest = rest[:7] + rest[6 + n_token :]
    role = rest[4][1]
    work = role == active[0]
    for other in active[1:]:
        work = work | (role == other)

    @pl.when(work)
    def _():
        meet_work(*rest)


def meet_work(n_src, gal_ids, scale3, topk, core_ref, live_ref, token_ref, *refs):
    n_gal = len(gal_ids)
    even = core_ref[0] == 0
    sources = [refs[i * (1 + 2 * n_gal) : (i + 1) * (1 + 2 * n_gal)] for i in range(n_src)]
    refs = refs[n_src * (1 + 2 * n_gal) :]
    gal_refs, refs = refs[:n_gal], refs[n_gal:]
    out_ref, w_ref = refs[:2]
    q_ref = sources[0][0]
    rows = q_ref.shape[0]
    if n_src == 2:
        far_ref, q_ref = sources[1][0], refs[2]

        @pl.when(even)
        def _():
            q_ref[...] = sources[0][0][...]

        @pl.when(jnp.logical_not(even))
        def _():
            q_ref[...] = far_ref[...]

    gal_rows, width = gal_refs[0].shape
    mass = jnp.zeros((rows, 128), jnp.float32)
    for g in range(n_gal):
        first, last = sources[0][1 + 2 * g], sources[-1][2 + 2 * g]
        if len(first.shape) == 3:
            picks = first[0]
        else:
            picks = jnp.where(even, unpack(first[...], topk), unpack(last[...], topk))
        pick, gain = pick_table(picks, live_ref[gal_ids[g]], scale3)
        for t in range(gal_rows // TILE):
            tile = gal_refs[g][t * TILE : (t + 1) * TILE, :]
            s = lax.dot_general(q_ref[...], tile, (((1,), (1,)), ((), ())), preferred_element_type=jnp.float32)
            col = lax.broadcasted_iota(jnp.int32, (rows, TILE), 1) + t * TILE
            c = jnp.zeros((rows, TILE), jnp.float32)
            for k in range(topk):
                c = jnp.where(col == pick[:, k : k + 1], gain[:, k : k + 1], c)
            r = jnp.maximum(s, 0.0)
            w = r * r * (r * c)
            for j in range(TILE // 128):
                mass = mass + w[:, j * 128 : (j + 1) * 128]
            w_ref[g, :, t * TILE : (t + 1) * TILE] = w.astype(jnp.bfloat16)
    for n in range(width // TILE):
        cut = slice(n * TILE, (n + 1) * TILE)
        total = jnp.dot(w_ref[0], gal_refs[0][:, cut], preferred_element_type=jnp.float32)
        for g in range(1, n_gal):
            total = total + jnp.dot(w_ref[g], gal_refs[g][:, cut], preferred_element_type=jnp.float32)
        out_ref[:rows, cut] = total.astype(out_ref.dtype)
    mass = jnp.sum(mass.T, axis=0, keepdims=True)
    high = mass.astype(jnp.bfloat16).astype(jnp.float32)
    mid = (mass - high).astype(jnp.bfloat16).astype(jnp.float32)
    part = lax.broadcasted_iota(jnp.int32, (TAIL, rows), 0)
    tail = jnp.where(part == 0, high, jnp.where(part == 1, mid, jnp.where(part == 2, mass - high - mid, 0.0)))
    out_ref[rows:, :] = jnp.zeros((TAIL, width), out_ref.dtype)
    out_ref[rows:, :rows] = tail.astype(out_ref.dtype)


def meet(core, lives, tokens, sources, gals, steps, rows, at, topk, active=(0, 1, 2)):
    gal_rows, width = gals[0].shape
    n_gal = len(gals)
    operands, specs = [], []
    for source in sources:
        raw = isinstance(source, tuple)
        queries = source[0] if raw else source
        operands.append(queries)
        specs.append(pl.BlockSpec((rows, width), functools.partial(lambda o, i: (o, 0), at if raw else 0)))
        for _, *both in steps:
            for step in both:
                if raw:
                    operands.append(source[1])
                    specs.append(pl.BlockSpec((1, topk, rows), functools.partial(lambda s, i: (s, 0, at), step)))
                else:
                    operands.append(queries)
                    specs.append(
                        pl.BlockSpec((TAIL, rows), functools.partial(lambda s, i: (rows // TAIL, s), step))
                    )
    scratch = [pltpu.VMEM((n_gal, rows, gal_rows), jnp.bfloat16)]
    if len(sources) == 2:
        scratch.append(pltpu.VMEM((rows, width), jnp.bfloat16))
    return pl.pallas_call(
        functools.partial(meet_kernel, active, len(tokens), len(sources), tuple(s[0] for s in steps), float(width) ** -1.5, topk),
        grid=(1,),
        out_shape=jax.ShapeDtypeStruct((rows + TAIL, width), jnp.bfloat16),
        in_specs=[
            pl.BlockSpec(memory_space=pltpu.SMEM),
            pl.BlockSpec(memory_space=pltpu.SMEM),
        ]
        + [pl.BlockSpec(memory_space=pl.ANY)] * len(tokens)
        + specs
        + [pl.BlockSpec((gal_rows, width), lambda i: (0, 0))] * n_gal,
        out_specs=pl.BlockSpec((rows + TAIL, width), lambda i: (0, 0)),
        scratch_shapes=scratch,
        compiler_params=pltpu.CompilerParams(vmem_limit_bytes=VMEM_BYTES),
        cost_estimate=cost(rows * width),
    )(core, lives, *tokens, *operands, *gals)


def after_kernel(x_ref, other_ref, out_ref):
    pass


def after(x, other):
    return pl.pallas_call(
        after_kernel,
        out_shape=jax.ShapeDtypeStruct(x.shape, x.dtype),
        in_specs=[pl.BlockSpec(memory_space=pl.ANY)] * 2,
        out_specs=pl.BlockSpec(memory_space=pl.ANY),
        input_output_aliases={0: 0},
        compiler_params=pltpu.CompilerParams(vmem_limit_bytes=VMEM_BYTES),
        cost_estimate=cost(1),
    )(x, other)


def gather_kernel(q_ref, own_ref, near_ref, token_ref, out_ref):
    out_ref[...] = q_ref[...].astype(jnp.float32) + (own_ref[...].astype(jnp.float32) + near_ref[...].astype(jnp.float32))


def gather(at, rows, queries, own, near, token, block=128):
    width = queries.shape[1]
    first = at * rows // block
    here = pl.BlockSpec((block, width), lambda i: (first + i, 0))
    alone = pl.BlockSpec((block, width), lambda i: (i, 0))
    return pl.pallas_call(
        gather_kernel,
        grid=(rows // block,),
        out_shape=jax.ShapeDtypeStruct((rows, width), jnp.float32),
        in_specs=[here, here, alone, pl.BlockSpec(memory_space=pl.ANY)],
        out_specs=alone,
        compiler_params=pltpu.CompilerParams(vmem_limit_bytes=VMEM_BYTES),
        cost_estimate=cost(64 * rows * width),
    )(queries, own, near, token)


def finish_kernel(block, flag_ref, sum_ref, own_tail, near_tail, *refs):
    out_ref = refs[-1]
    part = lax.rem(pl.program_id(0), 128 // block)

    def write(far_ref, far_tail):
        tails = own_tail[...].astype(jnp.float32) + near_tail[...].astype(jnp.float32) + far_tail[...].astype(jnp.float32)
        share = 1.0 / (1.0 + jnp.sum(tails.T, axis=1, keepdims=True))
        mine = share[:block]
        for p in range(1, 128 // block):
            mine = jnp.where(part == p, share[p * block : (p + 1) * block], mine)
        out_ref[...] = ((sum_ref[...] + far_ref[...].astype(jnp.float32)) * mine).astype(out_ref.dtype)

    for role in range(3):
        pl.when(flag_ref[1] == role)(functools.partial(write, refs[2 * role], refs[2 * role + 1]))


def finish(flags, at, rows, all_rows, sums, own, near, fars, done, block=128):
    width = sums.shape[1]
    first = at * rows // block
    alone = pl.BlockSpec((block, width), lambda i: (i, 0))

    def tail(array, begin):
        row = (array.shape[0] - TAIL) // TAIL
        return pl.BlockSpec((TAIL, 128), lambda i: (row, (begin + i) * block // 128))

    operands = [flags, sums, own, near]
    specs = [pl.BlockSpec(memory_space=pltpu.SMEM), alone, tail(own, first), tail(near, 0)]
    for far in fars:
        operands += [far, far]
        specs += [alone, tail(far, 0)]
    return pl.pallas_call(
        functools.partial(finish_kernel, block),
        grid=(rows // block,),
        out_shape=jax.ShapeDtypeStruct((all_rows, width), jnp.bfloat16),
        in_specs=specs + [pl.BlockSpec(memory_space=pl.ANY)],
        out_specs=pl.BlockSpec((block, width), lambda i: (first + i, 0)),
        compiler_params=pltpu.CompilerParams(vmem_limit_bytes=VMEM_BYTES),
        cost_estimate=cost(64 * rows * width),
        **({"input_output_aliases": {len(operands): 0}} if at > 0 else {}),
    )(*operands, done)


def on_device(queries, gallery, neighbors, counts):
    n = lax.axis_size("blk")
    me = lax.axis_index("blk").astype(jnp.int32)
    core = jnp.stack([me % 2, (me % 2) * (1 + me % 4 // 2)])
    rows, width = queries.shape
    topk = neighbors.shape[2]
    picks = jnp.transpose(neighbors, (1, 2, 0))

    def shift(k):
        return [(i, (i + k) % n) for i in range(n)]

    def far_shift(k, *roles):
        return [(i, (i + k) % n) for i in range(n) if i % 2 and 1 + i % 4 // 2 in roles]

    swap = [(i, i ^ 1) for i in range(n)]

    size = rows // CHUNKS
    packed = [pack(queries, picks, counts, c * size, size) for c in range(CHUNKS)]
    early = lax.ppermute(packed[0], "blk", far_shift(4, 1))
    near = [lax.ppermute(chunk, "blk", shift(2)) for chunk in packed]
    other = lax.ppermute(gallery, "blk", swap)
    live = jnp.concatenate([counts, lax.ppermute(counts, "blk", swap)])

    token = packed[-1]
    far_step = ((1, 1, 3),)
    token = meet(core, live, [token], [packed[0], early], (other,), far_step, size, 0, topk, (0, 1))
    far_here = [token]
    early_back = lax.ppermute(token, "blk", far_shift(-4, 1))
    late = []
    for c in range(CHUNKS):
        token = pack(queries, picks, token, c * size, size)
        late.append(lax.ppermute(token, "blk", far_shift(4, 1, 2) if c else far_shift(4, 2)))
    near_back = []
    for c in range(CHUNKS):
        token = meet(core, live, [token], [near[c]], (gallery, other), ((0, 2, 2), (1, 3, 1)), size, 0, topk)
        token = after(token, near[-1]) if c + 1 < CHUNKS else token
        near_back.append(lax.ppermute(token, "blk", shift(-2)))
    token = meet(core, live, [token, early_back], [packed[0], late[0]], (other,), far_step, size, 0, topk, (2,))
    fars = [(far_here[0], early_back, lax.ppermute(token, "blk", far_shift(-4, 2)))]
    for c in range(1, CHUNKS):
        token = meet(core, live, [token], [packed[c], late[c]], (other,), far_step, size, 0, topk)
        back = lax.ppermute(token, "blk", far_shift(-4, 1, 2))
        fars.append((token, back, back))
    own = meet(core, counts, [token], [(queries, picks)], (gallery,), ((0, 0, 0),), rows, 0, topk)
    token = own
    sums, mark = [], token
    for c in range(CHUNKS):
        mark = gather(c, size, queries, own, near_back[c], mark)
        sums.append(mark)
    done = mark
    for c in range(CHUNKS):
        done = finish(core, c, size, rows, sums[c], own, near_back[c], fars[c], done)
    return done


def solution(mesh):
    return jax.shard_map(
        on_device,
        mesh=mesh,
        in_specs=(
            P(("groups", "blk"), None),
            P(("groups", "blk"), None),
            P(("groups", "blk"), None, None),
            P(("groups", "blk")),
        ),
        out_specs=P(("groups", "blk"), None),
        check_vma=False,
    )
```

```python
import functools

import jax
import jax.numpy as jnp
from jax import lax
from jax.experimental import pallas as pl
from jax.experimental.pallas import tpu as pltpu
from jax.sharding import PartitionSpec as P

CHUNKS = 2
TILE = 256
TAIL = 16
BASE = 256
VMEM_BYTES = 65000 * 1024


def cost(flops):
    return pl.CostEstimate(flops=flops, bytes_accessed=flops // 64, transcendentals=0)


def pack_kernel(q_ref, picks_ref, token_ref, out_ref):
    steps, topk, rows = picks_ref.shape
    out_ref[:rows, :] = q_ref[...]
    out_ref[rows:, :] = jnp.zeros((TAIL, out_ref.shape[1]), out_ref.dtype)
    for s in range(steps):
        picks = picks_ref[s]
        halves = [(picks >> 8).astype(jnp.float32), (picks & (BASE - 1)).astype(jnp.float32)]
        out_ref[rows:, s * rows : (s + 1) * rows] = jnp.concatenate(halves, axis=0).astype(out_ref.dtype)


def pack(queries, picks, token, first, rows):
    width = queries.shape[1]
    at = first // rows
    return pl.pallas_call(
        pack_kernel,
        grid=(1,),
        out_shape=jax.ShapeDtypeStruct((rows + TAIL, width), queries.dtype),
        in_specs=[
            pl.BlockSpec((rows, width), lambda i: (at, 0)),
            pl.BlockSpec((*picks.shape[:2], rows), lambda i: (0, 0, at)),
            pl.BlockSpec(memory_space=pl.ANY),
        ],
        out_specs=pl.BlockSpec((rows + TAIL, width), lambda i: (0, 0)),
        compiler_params=pltpu.CompilerParams(vmem_limit_bytes=VMEM_BYTES),
        cost_estimate=cost(rows * width),
    )(queries, picks, token)


def unpack(tail, topk):
    parts = tail.astype(jnp.float32)
    return (parts[:topk] * BASE + parts[topk:]).astype(jnp.int32)


def pick_table(picks, live, scale3):
    topk = picks.shape[0]
    place = lax.broadcasted_iota(jnp.int32, picks.shape, 0)
    many = jnp.ones(picks.shape, jnp.float32)
    keep = picks < live
    for turn in range(1, topk):
        same = picks == pltpu.roll(picks, turn, 0)
        many = many + jnp.where(same, 1.0, 0.0)
        keep = keep & jnp.logical_not(same & (place >= turn))
    return jnp.where(keep, picks, -1).T, (many * scale3).T


def meet_kernel(active, n_token, carry, *rest):
    rest = rest[:7] + rest[6 + n_token :]
    role = rest[4][1]
    work = role == active[0]
    for other in active[1:]:
        work = work | (role == other)

    @pl.when(work)
    def _():
        meet_work(carry, *rest)


def meet_work(carry, n_src, gal_ids, scale3, topk, core_ref, live_ref, token_ref, *refs):
    n_gal = len(gal_ids)
    even = core_ref[0] == 0
    sources = [refs[i * (1 + 2 * n_gal) : (i + 1) * (1 + 2 * n_gal)] for i in range(n_src)]
    refs = refs[n_src * (1 + 2 * n_gal) :]
    gal_refs, refs = refs[:n_gal], refs[n_gal:]
    before_ref = tail_ref = None
    if carry == "in":
        before_ref, *refs = refs
    out_ref, *refs = refs
    if carry == "out":
        tail_ref, *refs = refs
    w_ref, *refs = refs
    q_ref = sources[0][0]
    rows = q_ref.shape[0]
    if n_src == 2:
        far_ref, q_ref = sources[1][0], refs[0]

        @pl.when(even)
        def _():
            q_ref[...] = sources[0][0][...]

        @pl.when(jnp.logical_not(even))
        def _():
            q_ref[...] = far_ref[...]

    gal_rows, width = gal_refs[0].shape
    mass = jnp.zeros((rows, 128), jnp.float32)
    for g in range(n_gal):
        first, last = sources[0][1 + 2 * g], sources[-1][2 + 2 * g]
        if len(first.shape) == 3:
            picks = first[0]
        else:
            picks = jnp.where(even, unpack(first[...], topk), unpack(last[...], topk))
        pick, gain = pick_table(picks, live_ref[gal_ids[g]], scale3)
        for t in range(gal_rows // TILE):
            tile = gal_refs[g][t * TILE : (t + 1) * TILE, :]
            s = lax.dot_general(q_ref[...], tile, (((1,), (1,)), ((), ())), preferred_element_type=jnp.float32)
            col = lax.broadcasted_iota(jnp.int32, (rows, TILE), 1) + t * TILE
            c = jnp.zeros((rows, TILE), jnp.float32)
            for k in range(topk):
                c = jnp.where(col == pick[:, k : k + 1], gain[:, k : k + 1], c)
            r = jnp.maximum(s, 0.0)
            w = r * r * (r * c)
            for j in range(TILE // 128):
                mass = mass + w[:, j * 128 : (j + 1) * 128]
            w_ref[g, :, t * TILE : (t + 1) * TILE] = w.astype(jnp.bfloat16)
    for n in range(width // TILE):
        cut = slice(n * TILE, (n + 1) * TILE)
        total = jnp.dot(w_ref[0], gal_refs[0][:, cut], preferred_element_type=jnp.float32)
        for g in range(1, n_gal):
            total = total + jnp.dot(w_ref[g], gal_refs[g][:, cut], preferred_element_type=jnp.float32)
        out_ref[:rows, cut] = total.astype(out_ref.dtype)
    mass = jnp.sum(mass.T, axis=0, keepdims=True)
    high = mass.astype(jnp.bfloat16).astype(jnp.float32)
    mid = (mass - high).astype(jnp.bfloat16).astype(jnp.float32)
    part = lax.broadcasted_iota(jnp.int32, (TAIL, rows), 0)
    tail = jnp.where(part == 0, high, jnp.where(part == 1, mid, jnp.where(part == 2, mass - high - mid, 0.0)))
    tail = tail.astype(out_ref.dtype)
    if tail_ref is not None:
        tail_ref[...] = tail
        return
    out_ref[rows:, :] = jnp.zeros((TAIL, width), out_ref.dtype)
    begin = 0
    if before_ref is not None:
        begin = before_ref.shape[1]
        out_ref[rows:, :begin] = before_ref[...]
    out_ref[rows:, begin : begin + rows] = tail


def meet(core, lives, tokens, sources, gals, steps, rows, at, topk, active=(0, 1, 2), carry=None):
    gal_rows, width = gals[0].shape
    n_gal = len(gals)
    operands, specs = [], []
    for source in sources:
        raw = isinstance(source, tuple)
        queries = source[0] if raw else source
        operands.append(queries)
        specs.append(pl.BlockSpec((rows, width), functools.partial(lambda o, i: (o, 0), at if raw else 0)))
        for _, *both in steps:
            for step in both:
                if raw:
                    operands.append(source[1])
                    specs.append(pl.BlockSpec((1, topk, rows), functools.partial(lambda s, i: (s, 0, at), step)))
                else:
                    operands.append(queries)
                    specs.append(
                        pl.BlockSpec((TAIL, rows), functools.partial(lambda s, i: (rows // TAIL, s), step))
                    )
    mode = carry if carry is None or isinstance(carry, str) else "in"
    extra, extra_specs = ([carry], [pl.BlockSpec(carry.shape, lambda i: (0, 0))]) if mode == "in" else ([], [])
    high = rows + (0 if mode == "out" else TAIL)
    out_shape = [jax.ShapeDtypeStruct((high, width), jnp.bfloat16)]
    out_specs = [pl.BlockSpec((high, width), lambda i: (0, 0))]
    if mode == "out":
        out_shape.append(jax.ShapeDtypeStruct((TAIL, rows), jnp.bfloat16))
        out_specs.append(pl.BlockSpec((TAIL, rows), lambda i: (0, 0)))
    scratch = [pltpu.VMEM((n_gal, rows, gal_rows), jnp.bfloat16)]
    if len(sources) == 2:
        scratch.append(pltpu.VMEM((rows, width), jnp.bfloat16))
    results = pl.pallas_call(
        functools.partial(meet_kernel, active, len(tokens), mode, len(sources), tuple(s[0] for s in steps), float(width) ** -1.5, topk),
        grid=(1,),
        out_shape=out_shape,
        in_specs=[
            pl.BlockSpec(memory_space=pltpu.SMEM),
            pl.BlockSpec(memory_space=pltpu.SMEM),
        ]
        + [pl.BlockSpec(memory_space=pl.ANY)] * len(tokens)
        + specs
        + [pl.BlockSpec((gal_rows, width), lambda i: (0, 0))] * n_gal
        + extra_specs,
        out_specs=out_specs,
        scratch_shapes=scratch,
        compiler_params=pltpu.CompilerParams(vmem_limit_bytes=VMEM_BYTES),
        cost_estimate=cost(rows * width),
    )(core, lives, *tokens, *operands, *gals, *extra)
    return results if mode == "out" else results[0]


def after_kernel(x_ref, other_ref, out_ref):
    pass


def after(x, other):
    return pl.pallas_call(
        after_kernel,
        out_shape=jax.ShapeDtypeStruct(x.shape, x.dtype),
        in_specs=[pl.BlockSpec(memory_space=pl.ANY)] * 2,
        out_specs=pl.BlockSpec(memory_space=pl.ANY),
        input_output_aliases={0: 0},
        compiler_params=pltpu.CompilerParams(vmem_limit_bytes=VMEM_BYTES),
        cost_estimate=cost(1),
    )(x, other)


def gather_kernel(q_ref, own_ref, near_ref, token_ref, out_ref):
    out_ref[...] = q_ref[...].astype(jnp.float32) + (own_ref[...].astype(jnp.float32) + near_ref[...].astype(jnp.float32))


def gather(at, rows, queries, own, near, token, block=128):
    width = queries.shape[1]
    first = at * rows // block
    here = pl.BlockSpec((block, width), lambda i: (first + i, 0))
    alone = pl.BlockSpec((block, width), lambda i: (i, 0))
    return pl.pallas_call(
        gather_kernel,
        grid=(rows // block,),
        out_shape=jax.ShapeDtypeStruct((rows, width), jnp.float32),
        in_specs=[here, here, alone, pl.BlockSpec(memory_space=pl.ANY)],
        out_specs=alone,
        compiler_params=pltpu.CompilerParams(vmem_limit_bytes=VMEM_BYTES),
        cost_estimate=cost(8192 * rows * width),
    )(queries, own, near, token)


def finish_kernel(block, flag_ref, sum_ref, own_tail, near_tail, *refs):
    out_ref = refs[-1]
    part = lax.rem(pl.program_id(0), 128 // block)

    def write(far_ref, far_tail):
        tails = own_tail[...].astype(jnp.float32) + near_tail[...].astype(jnp.float32) + far_tail[...].astype(jnp.float32)
        share = 1.0 / (1.0 + jnp.sum(tails.T, axis=1, keepdims=True))
        mine = share[:block]
        for p in range(1, 128 // block):
            mine = jnp.where(part == p, share[p * block : (p + 1) * block], mine)
        out_ref[...] = ((sum_ref[...] + far_ref[...].astype(jnp.float32)) * mine).astype(out_ref.dtype)

    for role in range(3):
        pl.when(flag_ref[1] == role)(functools.partial(write, refs[2 * role], refs[2 * role + 1]))


def finish(flags, at, rows, all_rows, sums, own, near, fars, done, block=128):
    width = sums.shape[1]
    first = at * rows // block
    alone = pl.BlockSpec((block, width), lambda i: (i, 0))

    def tail(array, begin):
        row = (array.shape[0] - TAIL) // TAIL
        return pl.BlockSpec((TAIL, 128), lambda i: (row, (begin + i) * block // 128))

    operands = [flags, sums, own, near]
    specs = [pl.BlockSpec(memory_space=pltpu.SMEM), alone, tail(own, first), tail(near, first)]
    for far in fars:
        operands += [far, far]
        specs += [alone, tail(far, 0)]
    return pl.pallas_call(
        functools.partial(finish_kernel, block),
        grid=(rows // block,),
        out_shape=jax.ShapeDtypeStruct((all_rows, width), jnp.bfloat16),
        in_specs=specs + [pl.BlockSpec(memory_space=pl.ANY)],
        out_specs=pl.BlockSpec((block, width), lambda i: (first + i, 0)),
        compiler_params=pltpu.CompilerParams(vmem_limit_bytes=VMEM_BYTES),
        cost_estimate=cost(64 * rows * width),
        **({"input_output_aliases": {len(operands): 0}} if at > 0 else {}),
    )(*operands, done)


def on_device(queries, gallery, neighbors, counts):
    n = lax.axis_size("blk")
    me = lax.axis_index("blk").astype(jnp.int32)
    core = jnp.stack([me % 2, (me % 2) * (1 + me % 4 // 2)])
    rows, width = queries.shape
    topk = neighbors.shape[2]
    picks = jnp.transpose(neighbors, (1, 2, 0))

    def shift(k):
        return [(i, (i + k) % n) for i in range(n)]

    def far_shift(k, *roles):
        return [(i, (i + k) % n) for i in range(n) if i % 2 and 1 + i % 4 // 2 in roles]

    swap = [(i, i ^ 1) for i in range(n)]

    size = rows // CHUNKS
    packed = [pack(queries, picks, counts, c * size, size) for c in range(CHUNKS)]
    early = lax.ppermute(packed[0], "blk", far_shift(4, 1))
    near = [lax.ppermute(chunk, "blk", shift(2)) for chunk in packed]
    other = lax.ppermute(gallery, "blk", swap)
    live = jnp.concatenate([counts, lax.ppermute(counts, "blk", swap)])

    token = packed[-1]
    far_step = ((1, 1, 3),)
    token = meet(core, live, [token], [packed[0], early], (other,), far_step, size, 0, topk, (0, 1))
    far_here = [token]
    early_back = lax.ppermute(token, "blk", far_shift(-4, 1))
    late = []
    for c in range(CHUNKS):
        token = pack(queries, picks, token, c * size, size)
        late.append(lax.ppermute(token, "blk", far_shift(4, 1, 2) if c else far_shift(4, 2)))
    near_step = ((0, 2, 2), (1, 3, 1))
    total, tail = meet(core, live, [token], [near[0]], (gallery, other), near_step, size, 0, topk, carry="out")
    total = after(total, near[1])
    near_back = [lax.ppermute(total, "blk", shift(-2))]
    token = meet(core, live, [total], [near[1]], (gallery, other), near_step, size, 0, topk, carry=tail)
    near_back.append(lax.ppermute(token, "blk", shift(-2)))
    token = meet(core, live, [token, early_back], [packed[0], late[0]], (other,), far_step, size, 0, topk, (2,))
    fars = [(far_here[0], early_back, lax.ppermute(token, "blk", far_shift(-4, 2)))]
    for c in range(1, CHUNKS):
        token = meet(core, live, [token], [packed[c], late[c]], (other,), far_step, size, 0, topk)
        back = lax.ppermute(token, "blk", far_shift(-4, 1, 2))
        fars.append((token, back, back))
    own = meet(core, counts, [token], [(queries, picks)], (gallery,), ((0, 0, 0),), rows, 0, topk)
    token = own
    sums, mark = [], token
    for c in range(CHUNKS):
        mark = gather(c, size, queries, own, near_back[c], mark)
        sums.append(mark)
    done = mark
    for c in range(CHUNKS):
        done = finish(core, c, size, rows, sums[c], own, near_back[-1], fars[c], done)
    return done


def solution(mesh):
    return jax.shard_map(
        on_device,
        mesh=mesh,
        in_specs=(
            P(("groups", "blk"), None),
            P(("groups", "blk"), None),
            P(("groups", "blk"), None, None),
            P(("groups", "blk")),
        ),
        out_specs=P(("groups", "blk"), None),
        check_vma=False,
    )
```

```python
import functools

import jax
import jax.numpy as jnp
from jax import lax
from jax.experimental import pallas as pl
from jax.experimental.pallas import tpu as pltpu
from jax.sharding import PartitionSpec as P

CHUNKS = 2
TILE = 256
TAIL = 16
BASE = 256
VMEM_BYTES = 65000 * 1024


def cost(flops):
    return pl.CostEstimate(flops=flops, bytes_accessed=flops // 64, transcendentals=0)


def pack_kernel(q_ref, picks_ref, token_ref, out_ref):
    steps, topk, rows = picks_ref.shape
    out_ref[:rows, :] = q_ref[...]
    out_ref[rows:, :] = jnp.zeros((TAIL, out_ref.shape[1]), out_ref.dtype)
    for s in range(steps):
        picks = picks_ref[s]
        halves = [(picks >> 8).astype(jnp.float32), (picks & (BASE - 1)).astype(jnp.float32)]
        out_ref[rows:, s * rows : (s + 1) * rows] = jnp.concatenate(halves, axis=0).astype(out_ref.dtype)


def pack(queries, picks, token, first, rows):
    width = queries.shape[1]
    at = first // rows
    return pl.pallas_call(
        pack_kernel,
        grid=(1,),
        out_shape=jax.ShapeDtypeStruct((rows + TAIL, width), queries.dtype),
        in_specs=[
            pl.BlockSpec((rows, width), lambda i: (at, 0)),
            pl.BlockSpec((*picks.shape[:2], rows), lambda i: (0, 0, at)),
            pl.BlockSpec(memory_space=pl.ANY),
        ],
        out_specs=pl.BlockSpec((rows + TAIL, width), lambda i: (0, 0)),
        compiler_params=pltpu.CompilerParams(vmem_limit_bytes=VMEM_BYTES),
        cost_estimate=cost(rows * width),
    )(queries, picks, token)


def unpack(tail, topk):
    parts = tail.astype(jnp.float32)
    return (parts[:topk] * BASE + parts[topk:]).astype(jnp.int32)


def pick_table(picks, live, scale3):
    topk = picks.shape[0]
    place = lax.broadcasted_iota(jnp.int32, picks.shape, 0)
    many = jnp.ones(picks.shape, jnp.float32)
    keep = picks < live
    for turn in range(1, topk):
        same = picks == pltpu.roll(picks, turn, 0)
        many = many + jnp.where(same, 1.0, 0.0)
        keep = keep & jnp.logical_not(same & (place >= turn))
    return jnp.where(keep, picks, -1).T, (many * scale3).T


def meet_kernel(active, n_token, carry, *rest):
    rest = rest[:7] + rest[6 + n_token :]
    role = rest[4][1]
    work = role == active[0]
    for other in active[1:]:
        work = work | (role == other)

    @pl.when(work)
    def _():
        meet_work(carry, *rest)


def meet_work(carry, n_src, gal_ids, scale3, topk, core_ref, live_ref, token_ref, *refs):
    n_gal = len(gal_ids)
    even = core_ref[0] == 0
    sources = [refs[i * (1 + 2 * n_gal) : (i + 1) * (1 + 2 * n_gal)] for i in range(n_src)]
    refs = refs[n_src * (1 + 2 * n_gal) :]
    gal_refs, refs = refs[:n_gal], refs[n_gal:]
    before_ref = tail_ref = None
    if carry == "in":
        before_ref, *refs = refs
    out_ref, *refs = refs
    if carry == "out":
        tail_ref, *refs = refs
    w_ref, *refs = refs
    q_ref = sources[0][0]
    rows = q_ref.shape[0]
    if n_src == 2:
        far_ref, q_ref = sources[1][0], refs[0]

        @pl.when(even)
        def _():
            q_ref[...] = sources[0][0][...]

        @pl.when(jnp.logical_not(even))
        def _():
            q_ref[...] = far_ref[...]

    gal_rows, width = gal_refs[0].shape
    mass = jnp.zeros((rows, 128), jnp.float32)
    for g in range(n_gal):
        first, last = sources[0][1 + 2 * g], sources[-1][2 + 2 * g]
        if len(first.shape) == 3:
            picks = first[0]
        else:
            picks = jnp.where(even, unpack(first[...], topk), unpack(last[...], topk))
        pick, gain = pick_table(picks, live_ref[gal_ids[g]], scale3)
        for t in range(gal_rows // TILE):
            tile = gal_refs[g][t * TILE : (t + 1) * TILE, :]
            s = lax.dot_general(q_ref[...], tile, (((1,), (1,)), ((), ())), preferred_element_type=jnp.float32)
            col = lax.broadcasted_iota(jnp.int32, (rows, TILE), 1) + t * TILE
            c = jnp.zeros((rows, TILE), jnp.float32)
            for k in range(topk):
                c = jnp.where(col == pick[:, k : k + 1], gain[:, k : k + 1], c)
            r = jnp.maximum(s, 0.0)
            w = r * r * (r * c)
            for j in range(TILE // 128):
                mass = mass + w[:, j * 128 : (j + 1) * 128]
            w_ref[g, :, t * TILE : (t + 1) * TILE] = w.astype(jnp.bfloat16)
    for n in range(width // TILE):
        cut = slice(n * TILE, (n + 1) * TILE)
        total = jnp.dot(w_ref[0], gal_refs[0][:, cut], preferred_element_type=jnp.float32)
        for g in range(1, n_gal):
            total = total + jnp.dot(w_ref[g], gal_refs[g][:, cut], preferred_element_type=jnp.float32)
        out_ref[:rows, cut] = total.astype(out_ref.dtype)
    mass = jnp.sum(mass.T, axis=0, keepdims=True)
    high = mass.astype(jnp.bfloat16).astype(jnp.float32)
    mid = (mass - high).astype(jnp.bfloat16).astype(jnp.float32)
    part = lax.broadcasted_iota(jnp.int32, (TAIL, rows), 0)
    tail = jnp.where(part == 0, high, jnp.where(part == 1, mid, jnp.where(part == 2, mass - high - mid, 0.0)))
    tail = tail.astype(out_ref.dtype)
    if tail_ref is not None:
        tail_ref[...] = tail
        return
    out_ref[rows:, :] = jnp.zeros((TAIL, width), out_ref.dtype)
    begin = 0
    if before_ref is not None:
        begin = before_ref.shape[1]
        out_ref[rows:, :begin] = before_ref[...]
    out_ref[rows:, begin : begin + rows] = tail


def meet(core, lives, tokens, sources, gals, steps, rows, at, topk, active=(0, 1, 2), carry=None):
    gal_rows, width = gals[0].shape
    n_gal = len(gals)
    operands, specs = [], []
    for source in sources:
        raw = isinstance(source, tuple)
        queries = source[0] if raw else source
        operands.append(queries)
        specs.append(pl.BlockSpec((rows, width), functools.partial(lambda o, i: (o, 0), at if raw else 0)))
        for _, *both in steps:
            for step in both:
                if raw:
                    operands.append(source[1])
                    specs.append(pl.BlockSpec((1, topk, rows), functools.partial(lambda s, i: (s, 0, at), step)))
                else:
                    operands.append(queries)
                    specs.append(
                        pl.BlockSpec((TAIL, rows), functools.partial(lambda s, i: (rows // TAIL, s), step))
                    )
    mode = carry if carry is None or isinstance(carry, str) else "in"
    extra, extra_specs = ([carry], [pl.BlockSpec(carry.shape, lambda i: (0, 0))]) if mode == "in" else ([], [])
    high = rows + (0 if mode == "out" else TAIL)
    out_shape = [jax.ShapeDtypeStruct((high, width), jnp.bfloat16)]
    out_specs = [pl.BlockSpec((high, width), lambda i: (0, 0))]
    if mode == "out":
        out_shape.append(jax.ShapeDtypeStruct((TAIL, rows), jnp.bfloat16))
        out_specs.append(pl.BlockSpec((TAIL, rows), lambda i: (0, 0)))
    scratch = [pltpu.VMEM((n_gal, rows, gal_rows), jnp.bfloat16)]
    if len(sources) == 2:
        scratch.append(pltpu.VMEM((rows, width), jnp.bfloat16))
    results = pl.pallas_call(
        functools.partial(meet_kernel, active, len(tokens), mode, len(sources), tuple(s[0] for s in steps), float(width) ** -1.5, topk),
        grid=(1,),
        out_shape=out_shape,
        in_specs=[
            pl.BlockSpec(memory_space=pltpu.SMEM),
            pl.BlockSpec(memory_space=pltpu.SMEM),
        ]
        + [pl.BlockSpec(memory_space=pl.ANY)] * len(tokens)
        + specs
        + [pl.BlockSpec((gal_rows, width), lambda i: (0, 0))] * n_gal
        + extra_specs,
        out_specs=out_specs,
        scratch_shapes=scratch,
        compiler_params=pltpu.CompilerParams(vmem_limit_bytes=VMEM_BYTES),
        cost_estimate=cost(rows * width),
    )(core, lives, *tokens, *operands, *gals, *extra)
    return results if mode == "out" else results[0]


def after_kernel(x_ref, other_ref, out_ref):
    pass


def after(x, other):
    return pl.pallas_call(
        after_kernel,
        out_shape=jax.ShapeDtypeStruct(x.shape, x.dtype),
        in_specs=[pl.BlockSpec(memory_space=pl.ANY)] * 2,
        out_specs=pl.BlockSpec(memory_space=pl.ANY),
        input_output_aliases={0: 0},
        compiler_params=pltpu.CompilerParams(vmem_limit_bytes=VMEM_BYTES),
        cost_estimate=cost(1),
    )(x, other)


def gather_kernel(q_ref, own_ref, near_ref, token_ref, out_ref):
    out_ref[...] = q_ref[...].astype(jnp.float32) + (own_ref[...].astype(jnp.float32) + near_ref[...].astype(jnp.float32))


def gather(at, rows, queries, own, near, token, block=128):
    width = queries.shape[1]
    first = at * rows // block
    here = pl.BlockSpec((block, width), lambda i: (first + i, 0))
    alone = pl.BlockSpec((block, width), lambda i: (i, 0))
    return pl.pallas_call(
        gather_kernel,
        grid=(rows // block,),
        out_shape=jax.ShapeDtypeStruct((rows, width), jnp.float32),
        in_specs=[here, here, alone, pl.BlockSpec(memory_space=pl.ANY)],
        out_specs=alone,
        compiler_params=pltpu.CompilerParams(vmem_limit_bytes=VMEM_BYTES),
        cost_estimate=cost(8192 * rows * width),
    )(queries, own, near, token)


def finish_kernel(block, sources, flag_ref, sum_ref, own_tail, near_tail, *refs):
    out_ref = refs[-1]
    part = lax.rem(pl.program_id(0), 128 // block)

    def write(far_ref, far_tail):
        tails = own_tail[...].astype(jnp.float32) + near_tail[...].astype(jnp.float32) + far_tail[...].astype(jnp.float32)
        share = 1.0 / (1.0 + jnp.sum(tails.T, axis=1, keepdims=True))
        mine = share[:block]
        for p in range(1, 128 // block):
            mine = jnp.where(part == p, share[p * block : (p + 1) * block], mine)
        out_ref[...] = ((sum_ref[...] + far_ref[...].astype(jnp.float32)) * mine).astype(out_ref.dtype)

    for role in range(3):
        pl.when(flag_ref[1] == role)(functools.partial(write, refs[2 * sources[role]], refs[2 * sources[role] + 1]))


def finish(flags, at, rows, all_rows, sums, own, near, fars, done, block=128):
    width = sums.shape[1]
    first = at * rows // block
    alone = pl.BlockSpec((block, width), lambda i: (i, 0))

    def tail(array, begin):
        row = (array.shape[0] - TAIL) // TAIL
        return pl.BlockSpec((TAIL, 128), lambda i: (row, (begin + i) * block // 128))

    operands = [flags, sums, own, near]
    specs = [pl.BlockSpec(memory_space=pltpu.SMEM), alone, tail(own, first), tail(near, first)]
    distinct = [far for i, far in enumerate(fars) if not any(far is other for other in fars[:i])]
    sources = tuple(next(i for i, other in enumerate(distinct) if other is far) for far in fars)
    for far in distinct:
        operands += [far, far]
        specs += [alone, tail(far, 0)]
    return pl.pallas_call(
        functools.partial(finish_kernel, block, sources),
        grid=(rows // block,),
        out_shape=jax.ShapeDtypeStruct((all_rows, width), jnp.bfloat16),
        in_specs=specs + [pl.BlockSpec(memory_space=pl.ANY)],
        out_specs=pl.BlockSpec((block, width), lambda i: (first + i, 0)),
        compiler_params=pltpu.CompilerParams(vmem_limit_bytes=VMEM_BYTES),
        cost_estimate=cost(64 * rows * width),
        **({"input_output_aliases": {len(operands): 0}} if at > 0 else {}),
    )(*operands, done)


def on_device(queries, gallery, neighbors, counts):
    n = lax.axis_size("blk")
    me = lax.axis_index("blk").astype(jnp.int32)
    core = jnp.stack([me % 2, (me % 2) * (1 + me % 4 // 2)])
    rows, width = queries.shape
    topk = neighbors.shape[2]
    picks = jnp.transpose(neighbors, (1, 2, 0))

    def shift(k):
        return [(i, (i + k) % n) for i in range(n)]

    def far_shift(k, *roles):
        return [(i, (i + k) % n) for i in range(n) if i % 2 and 1 + i % 4 // 2 in roles]

    swap = [(i, i ^ 1) for i in range(n)]

    size = rows // CHUNKS
    packed = [pack(queries, picks, counts, c * size, size) for c in range(CHUNKS)]
    early = lax.ppermute(packed[0], "blk", far_shift(4, 1))
    near = [lax.ppermute(chunk, "blk", shift(2)) for chunk in packed]
    other = lax.ppermute(gallery, "blk", swap)
    live = jnp.concatenate([counts, lax.ppermute(counts, "blk", swap)])

    token = packed[-1]
    far_step = ((1, 1, 3),)
    token = meet(core, live, [token], [packed[0], early], (other,), far_step, size, 0, topk, (0, 1))
    far_here = [token]
    early_back = lax.ppermute(token, "blk", far_shift(-4, 1))
    late = []
    for c in range(CHUNKS):
        token = pack(queries, picks, token, c * size, size)
        late.append(lax.ppermute(token, "blk", far_shift(4, 1, 2) if c else far_shift(4, 2)))
    near_step = ((0, 2, 2), (1, 3, 1))
    total, tail = meet(core, live, [token], [near[0]], (gallery, other), near_step, size, 0, topk, carry="out")
    total = after(total, near[1])
    near_back = [lax.ppermute(total, "blk", shift(-2))]
    token = meet(core, live, [total], [near[1]], (gallery, other), near_step, size, 0, topk, carry=tail)
    near_back.append(lax.ppermute(token, "blk", shift(-2)))
    token = meet(core, live, [token, early_back], [packed[0], late[0]], (other,), far_step, size, 0, topk, (2,))
    fars = [(far_here[0], early_back, lax.ppermute(token, "blk", far_shift(-4, 2)))]
    for c in range(1, CHUNKS):
        token = meet(core, live, [token], [packed[c], late[c]], (other,), far_step, size, 0, topk)
        back = lax.ppermute(token, "blk", far_shift(-4, 1, 2))
        fars.append((token, back, back))
    own = meet(core, counts, [token], [(queries, picks)], (gallery,), ((0, 0, 0),), rows, 0, topk)
    token = own
    sums, mark = [], token
    for c in range(CHUNKS):
        mark = gather(c, size, queries, own, near_back[c], mark)
        sums.append(mark)
    done = mark
    for c in range(CHUNKS):
        done = finish(core, c, size, rows, sums[c], own, near_back[-1], fars[c], done)
    return done


def solution(mesh):
    return jax.shard_map(
        on_device,
        mesh=mesh,
        in_specs=(
            P(("groups", "blk"), None),
            P(("groups", "blk"), None),
            P(("groups", "blk"), None, None),
            P(("groups", "blk")),
        ),
        out_specs=P(("groups", "blk"), None),
        check_vma=False,
    )
```
